256 devices in a mesh: dp: 8 (over y, core), tensor: 32 (over x, z).
Axes of the slice: x: 4, y: 4, z: 8, core: 2. Of those that a mesh axis runs over, the one named last changes fastest.
Arguments:
- grad: bfloat16 [8, 3584, 9472], P('dp', 'tensor'), may hold values from -70 to 70
- error: float32 [8, 3584, 9472], P('dp', 'tensor'), may hold values from -3 to 3
- q_init: float32 [8, 9472], replicated, may hold values from -4 to 4
Outputs:
- decompressed: bfloat16 [3584, 9472], P('tensor')
- new_error: float32 [8, 3584, 9472], P('dp', 'tensor')
- q_next: float32 [8, 9472], replicated
The draws below stay inside these ranges and needn't reach their ends.
All inputs are finite; a program needn't handle non-finite values.
Results may differ from the reference program's by a relative error of at most 0.0025.
Values sent between devices are 32-bit elements; how exact they have to be, the bound alone decides.
A program may use at most 64 MiB of HBM per device.

```python
import jax
import jax.numpy as jnp
from jax import lax

ROWS = 3584
COLS = 9472
RANK = 8
ITERS = 4
N_DP = 8


def draw_grad(key, part):
    key = jax.random.fold_in(key, 11)
    keys = jax.random.split(key, 3)
    position = jnp.arange(ROWS, dtype=jnp.float32) / ROWS
    row_scale = jnp.exp(jnp.log(3.0) * (position - 0.5) + jnp.log(10.0) * (jax.random.uniform(keys[0], (ROWS,)) - 0.5))
    col_scale = jnp.exp(jnp.log(10.0) * (jax.random.uniform(keys[1], (COLS,)) - 0.5))
    values = jax.random.truncated_normal(keys[2], -4.0, 4.0, (N_DP, ROWS, COLS))
    values = values * row_scale[None, :, None] * col_scale[None, None, :]
    return jnp.clip(values, -70.0, 70.0).astype(jnp.bfloat16)


def block_scale(key, shape, shards, smallest, top_value):
    level, own = 1.0, jax.random.fold_in(key, 6)
    for axis_at, parts in shards:
        heights = jnp.exp(jax.random.uniform(jax.random.fold_in(own, axis_at), (parts,), jnp.float32, smallest / len(shards), top_value / len(shards)))
        level = level * jnp.repeat(heights, shape[axis_at] // parts).reshape([-1 if axis == axis_at else 1 for axis in range(len(shape))])
    return level


def gaussian(own_key, dims, width, bound, shards=(), kind=jnp.bfloat16):
    result = jax.random.normal(own_key, dims, jnp.float32) * width
    if len(shards) > 0:
        result = block_scale(own_key, dims, shards, -0.22, 0.18) * result
    return jnp.clip(result, min=-bound, max=bound).astype(kind)


def setup_inputs(seed: int = 0) -> dict:
    streams_of = jax.random.split(jax.random.key(seed), 4)
    grad = draw_grad(jax.random.fold_in(streams_of[3], 71), 0)
    error = gaussian(streams_of[1], (N_DP, ROWS, COLS), 0.5, 3.0, ((0, 8), (1, 32)), jnp.float32)
    q_init = gaussian(streams_of[2], (RANK, COLS), 1.0, 4.0, (), jnp.float32)
    return dict(grad=grad, error=error, q_init=q_init)


highest = lax.Precision.HIGHEST

def orthonormal(block, gram):
    factor = jnp.linalg.cholesky(gram)
    return lax.linalg.triangular_solve(factor, block, left_side=True, lower=True)

def reference(grad, error, q_init):
    merged = grad.astype(jnp.float32) + error
    q_hat = q_init
    for iteration in range(ITERS):
        p_sum = jnp.einsum('kc,drc->kr', q_hat, merged, precision=highest) / N_DP
        gram = jnp.dot(p_sum, p_sum.T, precision=highest)
        p_hat = orthonormal(p_sum, gram)
        q_sum = jnp.einsum('kr,drc->kc', p_hat, merged, precision=highest) / N_DP
        q_hat = q_sum
    approx = jnp.dot(p_hat.T, q_sum, precision=highest)
    return (approx.astype(jnp.bfloat16), merged - approx[None], q_sum)
```

```python
import jax
import jax.numpy as jnp
from jax import lax
from jax.experimental import pallas as pl
from jax.experimental.pallas import tpu as pltpu
from jax.sharding import PartitionSpec as P

MESH = pl.DeviceIdType.MESH
F32, BF16 = jnp.float32, jnp.bfloat16
ITERS = 4
RANK = 8
ROWS = 112
HALF = 56
COLS = 9472
LANE = 128
WIN = 640
STEP_Y = 18 * LANE
TOP = 32
PART = 24
CHUNK = 10 * LANE
STARTS = tuple(range(0, COLS, CHUNK))


def nt(a, b):
    return lax.dot_general(a, b, (((1,), (1,)), ((), ())), preferred_element_type=F32)


def nn(a, b):
    return lax.dot_general(a, b, (((1,), (0,)), ((), ())), preferred_element_type=F32)


def two_terms(a):
    high = a.astype(BF16).astype(F32)
    return high, a - high


def stacked(a):
    return jnp.concatenate(two_terms(a), axis=0).astype(BF16)


def inverse_factor(gram):
    shape = (RANK, LANE)
    row = lax.broadcasted_iota(jnp.int32, shape, 0)
    lane = lax.broadcasted_iota(jnp.int32, shape, 1)
    work = jnp.where(lane == row + RANK, 1.0, jnp.where(lane < RANK, gram, 0.0))
    for j in range(RANK - 1):
        scale = work[:, j : j + 1] / work[j : j + 1, j : j + 1]
        work = work - jnp.where(row > j, scale * work[j : j + 1, :], 0.0)
    diagonal = jnp.sum(jnp.where(lane == row, work, 0.0), axis=1, keepdims=True)
    return work[:, RANK : 2 * RANK] / jnp.sqrt(diagonal)


def apply(inverse, block):
    total = inverse[:, 0:1] * block[0:1, :]
    for j in range(1, RANK):
        total = total + inverse[:, j : j + 1] * block[j : j + 1, :]
    return total


def by_column(low, high):
    tiles = [
        jnp.concatenate([low[4 * i : 4 * i + 4], high[4 * i : 4 * i + 4]], axis=0)
        for i in range(6)
    ]
    return jnp.concatenate(tiles[:5], axis=1), tiles[5]


def power(
    grad, error, q_init, q_out, p_out,
    gbuf, m, qv, cr, ra, rb, fm, fp, sx, s, s_high, s_low,
    p1s, p1r, qs, cbuf, zs, zbuf, qall, ps, pbuf, pfin, qfin,
    lsem, csend, crecv, ysend, yrecv, xsem, p1sem, c1sem, zsem, c2sem, psem, fsem,
):
    d, t = lax.axis_index("dp"), lax.axis_index("tensor")
    y, c = d // 2, d % 2
    x, z = t // 8, t % 8

    def at(y_, c_, x_, z_):
        return (y_ * 2 + c_, x_ * 8 + z_)

    other = at(y, 1 - c, x, z)
    ahead_y, behind_y, far_y = (y + 1 + 2 * c) % 4, (y + 3 - 2 * c) % 4, (y + 2) % 4
    ahead, behind = at(ahead_y, c, x, z), at(behind_y, c, x, z)
    plane = [((y + j) % 4, (x + i) % 4) for i in range(4) for j in range(4)]
    plane_same = [at(yy, c, xx, z) for yy, xx in plane[1:]]
    plane_other = [at(yy, 1 - c, xx, z) for yy, xx in plane[1:]]
    line = [at(y, c, x, (z + k) % 8) for k in range(1, 8)]

    def remote(src, dst, send, recv, device):
        copy = pltpu.make_async_remote_copy(
            src, dst, send, recv, device_id=device, device_id_type=MESH
        )
        copy.start()

    def wait(ref, sem):
        pltpu.make_async_copy(ref, ref, sem).wait()

    barrier = pltpu.get_barrier_semaphore()
    partners = [other] + plane_same + plane_other + line
    for device in partners:
        pl.semaphore_signal(barrier, inc=1, device_id=device, device_id_type=MESH)

    n = len(STARTS)
    loads = []
    for i, start in enumerate(STARTS):
        columns = pl.ds(start, min(CHUNK, COLS - start))
        loads.append((
            pltpu.make_async_copy(grad.at[0, :, columns], gbuf.at[:, columns], lsem.at[i]),
            pltpu.make_async_copy(error.at[0, :, columns], m.at[:, columns], lsem.at[n + i]),
        ))
        for copy in loads[-1]:
            copy.start()
    q_load = pltpu.make_async_copy(q_init, qv, lsem.at[2 * n])
    q_load.start()
    for i, start in enumerate(STARTS):
        for copy in loads[i]:
            copy.wait()
        columns = pl.ds(start, min(CHUNK, COLS - start))
        m[:, columns] = gbuf[:, columns].astype(F32) + m[:, columns]
    q_load.wait()
    pl.semaphore_wait(barrier, len(partners))

    def window(yy, xx):
        return pl.ds(pl.multiple_of(yy * STEP_Y + xx * WIN, LANE), WIN)

    mine = pl.ds(pl.multiple_of(HALF * c, 8), HALF)
    theirs = pl.ds(pl.multiple_of(HALF * (1 - c), 8), HALF)
    order = [(x + 1 + j) % 4 for j in range(4)]
    for j in range(4):
        for yy in range(4):
            remote(m.at[theirs, window(yy, order[j])], cr.at[order[j], yy], csend.at[j], crecv.at[j], other)

    top, low = pl.ds(0, TOP), pl.ds(TOP, HALF - TOP)

    def first(j):
        xx = order[j]
        wait(cr.at[xx], crecv.at[j])
        cr[xx, far_y] = cr[xx, far_y] + m[mine, window(far_y, xx)]
        remote(cr.at[xx, far_y, top], ra.at[j], ysend.at[0, j], yrecv.at[0, j], ahead)
        remote(cr.at[xx, far_y, low], rb.at[j], ysend.at[1, j], yrecv.at[1, j], behind)
        cr[xx, ahead_y] = cr[xx, ahead_y] + m[mine, window(ahead_y, xx)]
        remote(cr.at[xx, ahead_y, low], fm.at[j, low], ysend.at[2, j], yrecv.at[2, j], ahead)
        cr[xx, behind_y] = cr[xx, behind_y] + m[mine, window(behind_y, xx)]
        remote(cr.at[xx, behind_y, top], fp.at[j, top], ysend.at[3, j], yrecv.at[3, j], behind)
        cr[xx, y] = cr[xx, y] + m[mine, window(y, xx)]

    def second(j):
        xx = order[j]
        wait(ra.at[j], yrecv.at[0, j])
        ra[j] = ra[j] + cr[xx, ahead_y, top]
        remote(ra.at[j], fm.at[j, top], ysend.at[4, j], yrecv.at[4, j], ahead)
        wait(rb.at[j], yrecv.at[1, j])
        rb[j] = rb[j] + cr[xx, behind_y, low]
        remote(rb.at[j], fp.at[j, low], ysend.at[5, j], yrecv.at[5, j], behind)

    here = pl.ds(pl.multiple_of(HALF * x, 8), HALF)

    def third(j):
        xx = order[j]
        wait(fm.at[j, low], yrecv.at[2, j])
        wait(fp.at[j, top], yrecv.at[3, j])
        wait(fm.at[j, top], yrecv.at[4, j])
        wait(fp.at[j, low], yrecv.at[5, j])
        total = (fm[j] + fp[j] + cr[xx, y]) * 0.125
        if j < 3:
            sx[j] = total
            remote(sx.at[j], s.at[here], xsem.at[0], xsem.at[1], at(y, c, xx, z))
        else:
            s[here] = total

    first(0)

    q_two = stacked(qv[...])
    p_term = jnp.zeros((RANK, ROWS), F32)
    for start in STARTS:
        stop = min(start + CHUNK, COLS)
        high, rest = two_terms(m[:, start:stop])
        q_part = q_two[:, start:stop]
        on_high = nt(q_part, high.astype(BF16))
        on_rest = nt(q_part, rest.astype(BF16))
        p_term = p_term + (on_high[:RANK] + on_high[RANK:]) + (on_rest[:RANK] + on_rest[RANK:])
    blank = jnp.zeros((RANK, LANE - HALF), F32)
    for half in range(2):
        p1s[half] = jnp.concatenate([p_term[:, HALF * half : HALF * half + HALF], blank], axis=1)
    place = x * 8 + d
    p1r[place] = p1s[c]
    for same, cross in zip(plane_same, plane_other):
        remote(p1s.at[c], p1r.at[place], p1sem.at[0], p1sem.at[1], same)
        remote(p1s.at[1 - c], p1r.at[place], p1sem.at[0], p1sem.at[1], cross)
    remote(p1s.at[1 - c], p1r.at[place], p1sem.at[0], p1sem.at[1], other)

    first(1)
    second(0)
    first(2)
    second(1)
    third(0)
    first(3)
    second(2)
    third(1)
    second(3)
    third(2)
    third(3)

    wait(p1r.at[pl.ds(0, 31)], p1sem.at[1])
    blocks = []
    for xx in range(4):
        total = p1r[8 * xx]
        for dd in range(1, 8):
            total = total + p1r[8 * xx + dd]
        blocks.append(total[:, :HALF])
    p_sum = jnp.concatenate(blocks, axis=1) * 0.125

    wait(s.at[pl.ds(0, 3 * HALF)], xsem.at[1])
    limit = jnp.where(jnp.logical_and(x == 3, y < 3), 3 * LANE, WIN)
    inside = lax.broadcasted_iota(jnp.int32, (4 * HALF, WIN), 1) < limit
    high, rest = two_terms(jnp.where(inside, s[...], 0.0))
    s_high[...] = high.astype(BF16)
    s_low[...] = rest.astype(BF16)

    own = pl.ds(pl.multiple_of(PART * c, 8), PART)
    cross = pl.ds(pl.multiple_of(PART * (1 - c), 8), PART)
    pad = jnp.zeros((RANK, LANE - RANK), F32)
    me = y * 4 + x
    for i in range(ITERS):
        last = i == ITERS - 1
        p_two = stacked(p_sum)
        a, b = nn(p_two, s_high[...]), nn(p_two, s_low[...])
        q_raw = (a[:RANK] + a[RANK:]) + (b[:RANK] + b[RANK:])
        gram = lax.dot_general(
            p_sum, p_sum, (((1,), (1,)), ((), ())),
            precision=lax.Precision.HIGHEST, preferred_element_type=F32,
        )
        gram = jnp.concatenate([gram, pad], axis=1)
        for half in range(2):
            ranks = slice(4 * half, 4 * half + 4)
            for k in range(5):
                qs[i, PART * half + 4 * k : PART * half + 4 * k + 4, :] = q_raw[ranks, LANE * k : LANE * k + LANE]
            qs[i, PART * half + 20 : PART * half + 24, :] = gram[ranks]
        remote(qs.at[i, cross], cbuf.at[i], c1sem.at[0, i], c1sem.at[1, i], other)
        if last:
            rows = jnp.zeros((RANK, HALF), F32)
            for xx in range(4):
                rows = jnp.where(x == xx, p_sum[:, HALF * xx : HALF * xx + HALF], rows)
            pfin[c] = jnp.concatenate([rows, blank], axis=1)
            remote(pfin.at[c], pfin.at[c], fsem.at[0], fsem.at[1], other)
        wait(cbuf.at[i], c1sem.at[1, i])
        zs[i] = qs[i, own] + cbuf[i]
        zbuf[i, z] = zs[i]
        for device in line:
            remote(zs.at[i], zbuf.at[i, z], zsem.at[0, i], zsem.at[1, i], device)
        wait(zbuf.at[i, pl.ds(0, 7)], zsem.at[1, i])
        total = zbuf[i, 0]
        for k in range(1, 8):
            total = total + zbuf[i, k]
        if last:
            break
        qall[i, own] = total
        remote(qall.at[i, own], qall.at[i, own], c2sem.at[0, i], c2sem.at[1, i], other)
        wait(qall.at[i, own], c2sem.at[1, i])
        q_raw, gram = by_column(qall[i, 0:PART, :], qall[i, PART : 2 * PART, :])
        q_two = stacked(q_raw)
        a, b = nt(q_two, s_high[...]), nt(q_two, s_low[...])
        p_raw = (a[:RANK] + a[RANK:]) + (b[:RANK] + b[RANK:])
        ps[i, 0:RANK, :] = p_raw[:, :LANE]
        ps[i, RANK : 2 * RANK, :] = jnp.concatenate(
            [p_raw[:, LANE:], jnp.zeros((RANK, 2 * LANE - 4 * HALF), F32)], axis=1
        )
        for device in plane_same:
            remote(ps.at[i], pbuf.at[i, me], psem.at[0, i], psem.at[1, i], device)
        pbuf[i, me] = ps[i]
        inverse = inverse_factor(gram)
        wait(pbuf.at[i, pl.ds(0, 15)], psem.at[1, i])
        p_raw = pbuf[i, 0]
        for k in range(1, 16):
            p_raw = p_raw + pbuf[i, k]
        p_raw = jnp.concatenate([p_raw[:RANK], p_raw[RANK:, : 4 * HALF - LANE]], axis=1)
        p_sum = apply(inverse, p_raw)

    slot = me * 2 + c
    qfin[slot] = total
    remote(qfin.at[slot], qfin.at[slot], fsem.at[2], fsem.at[3], other)
    for same, cross in zip(plane_same, plane_other):
        remote(qfin.at[slot], qfin.at[slot], fsem.at[4], fsem.at[5], same)
        remote(qfin.at[slot], qfin.at[slot], fsem.at[4], fsem.at[5], cross)
    wait(qfin.at[slot], fsem.at[3])
    wait(pfin.at[c], fsem.at[1])
    _, gram = by_column(qfin[me * 2], qfin[me * 2 + 1])
    inverse = inverse_factor(gram)
    p_hat = apply(inverse, jnp.concatenate([pfin[0][:, :HALF], pfin[1][:, :HALF]], axis=1))
    p_out[...] = jnp.concatenate([p_hat, jnp.zeros((RANK, LANE - ROWS), F32)], axis=1)
    wait(qfin.at[pl.ds(0, 30)], fsem.at[5])
    for yy in range(4):
        for xx in range(4):
            group = (yy * 4 + xx) * 2
            q_raw, _ = by_column(qfin[group], qfin[group + 1])
            width = 3 * LANE if xx == 3 and yy < 3 else WIN
            start = yy * STEP_Y + xx * WIN
            q_out[:, start : start + width] = apply(inverse, q_raw[:, :width])

    for j in range(4):
        wait(cr.at[j], csend.at[j])
        wait(ra.at[j], ysend.at[0, j])
        wait(rb.at[j], ysend.at[1, j])
        wait(fm.at[j, low], ysend.at[2, j])
        wait(fp.at[j, top], ysend.at[3, j])
        wait(ra.at[j], ysend.at[4, j])
        wait(rb.at[j], ysend.at[5, j])
    wait(sx, xsem.at[0])
    wait(p1r.at[pl.ds(0, 31)], p1sem.at[0])
    for i in range(ITERS):
        wait(cbuf.at[i], c1sem.at[0, i])
        wait(zbuf.at[i, pl.ds(0, 7)], zsem.at[0, i])
        if i < ITERS - 1:
            wait(cbuf.at[i], c2sem.at[0, i])
            wait(pbuf.at[i, pl.ds(0, 15)], psem.at[0, i])
    wait(pfin.at[0], fsem.at[0])
    wait(cbuf.at[0], fsem.at[2])
    wait(qfin.at[pl.ds(0, 30)], fsem.at[4])


def factors(grad, error, q_init):
    dma = pltpu.SemaphoreType.DMA
    vmem = pltpu.VMEM
    return pl.pallas_call(
        power,
        name="factors",
        out_shape=(
            jax.ShapeDtypeStruct((RANK, COLS), F32),
            jax.ShapeDtypeStruct((RANK, LANE), F32),
        ),
        in_specs=[pl.BlockSpec(memory_space=pl.ANY)] * 3,
        out_specs=(pl.BlockSpec(memory_space=vmem), pl.BlockSpec(memory_space=vmem)),
        scratch_shapes=[
            vmem((ROWS, COLS), BF16),
            vmem((ROWS, COLS), F32),
            vmem((RANK, COLS), F32),
            vmem((4, 4, HALF, WIN), F32),
            vmem((4, TOP, WIN), F32),
            vmem((4, HALF - TOP, WIN), F32),
            vmem((4, HALF, WIN), F32),
            vmem((4, HALF, WIN), F32),
            vmem((3, HALF, WIN), F32),
            vmem((4 * HALF, WIN), F32),
            vmem((4 * HALF, WIN), BF16),
            vmem((4 * HALF, WIN), BF16),
            vmem((2, RANK, LANE), F32),
            vmem((32, RANK, LANE), F32),
            vmem((ITERS, 2 * PART, LANE), F32),
            vmem((ITERS, PART, LANE), F32),
            vmem((ITERS, PART, LANE), F32),
            vmem((ITERS, 8, PART, LANE), F32),
            vmem((ITERS, 2 * PART, LANE), F32),
            vmem((ITERS, 2 * RANK, LANE), F32),
            vmem((ITERS, 16, 2 * RANK, LANE), F32),
            vmem((2, RANK, LANE), F32),
            vmem((32, PART, LANE), F32),
            dma((2 * len(STARTS) + 1,)),
            dma((4,)),
            dma((4,)),
            dma((6, 4)),
            dma((6, 4)),
            dma((2,)),
            dma((2,)),
            dma((2, ITERS)),
            dma((2, ITERS)),
            dma((2, ITERS)),
            dma((2, ITERS)),
            dma((6,)),
        ],
        compiler_params=pltpu.CompilerParams(
            collective_id=0, has_side_effects=True, vmem_limit_bytes=40 * 2**20
        ),
    )(grad, error, q_init)


def finish(p, q, grad, error, decompressed, new_error, q_next):
    p_high, p_rest = two_terms(p[:, :ROWS])
    q_high, q_rest = two_terms(q[...])
    left = jnp.concatenate([p_high, p_high, p_rest, p_rest], axis=0).astype(BF16)
    right = jnp.concatenate([q_high, q_rest, q_high, q_rest], axis=0).astype(BF16)
    approx = lax.dot_general(
        left, right, (((0,), (0,)), ((), ())), preferred_element_type=F32
    )
    decompressed[...] = approx.astype(BF16)
    new_error[...] = (grad[...].astype(F32) + error[...]) - approx
    q_next[...] = q[...]


def outputs(p_hat, q_sum, grad, error):
    def block(rows):
        return pl.BlockSpec((rows, CHUNK), lambda i: (0, i))

    whole = pl.BlockSpec((None, ROWS, CHUNK), lambda i: (0, 0, i))
    return pl.pallas_call(
        finish,
        name="outputs",
        grid=(len(STARTS),),
        in_specs=[pl.BlockSpec((RANK, LANE), lambda i: (0, 0)), block(RANK), whole, whole],
        out_specs=(block(ROWS), whole, block(RANK)),
        out_shape=(
            jax.ShapeDtypeStruct((ROWS, COLS), BF16),
            jax.ShapeDtypeStruct((1, ROWS, COLS), F32),
            jax.ShapeDtypeStruct((RANK, COLS), F32),
        ),
        compiler_params=pltpu.CompilerParams(vmem_limit_bytes=24 * 2**20),
    )(p_hat, q_sum, grad, error)


def local(grad, error, q_init):
    q_sum, p_hat = factors(grad, error, q_init)
    return outputs(p_hat, q_sum, grad, error)


def solution(mesh):
    return jax.shard_map(
        local,
        mesh=mesh,
        in_specs=(P("dp", "tensor", None), P("dp", "tensor", None), P()),
        out_specs=(P("tensor", None), P("dp", "tensor", None), P()),
        check_vma=False,
    )
```

```python
import jax
import jax.numpy as jnp
from jax import lax
from jax.experimental import pallas as pl
from jax.experimental.pallas import tpu as pltpu
from jax.sharding import PartitionSpec as P

MESH = pl.DeviceIdType.MESH
F32, BF16 = jnp.float32, jnp.bfloat16
ITERS = 4
RANK = 8
ROWS = 112
HALF = 56
SLOT = 64
COLS = 9472
LANE = 128
WIN = 640
STEP_Y = 18 * LANE
TOP = 32
PART = 24
CHUNK = 10 * LANE
STARTS = tuple(range(0, COLS, CHUNK))
PLANE = sorted(
    ((i, j) for i in range(4) for j in range(4) if i or j),
    key=lambda ij: -(min(ij[0], 4 - ij[0]) + min(ij[1], 4 - ij[1])),
)


def nt(a, b):
    return lax.dot_general(a, b, (((1,), (1,)), ((), ())), preferred_element_type=F32)


def nn(a, b):
    return lax.dot_general(a, b, (((1,), (0,)), ((), ())), preferred_element_type=F32)


def two_terms(a):
    high = a.astype(BF16).astype(F32)
    return high, a - high


def stacked(a):
    return jnp.concatenate(two_terms(a), axis=0).astype(BF16)


def inverse_factor(gram):
    shape = (RANK, LANE)
    row = lax.broadcasted_iota(jnp.int32, shape, 0)
    lane = lax.broadcasted_iota(jnp.int32, shape, 1)
    work = jnp.where(lane == row + RANK, 1.0, jnp.where(lane < RANK, gram, 0.0))
    for j in range(RANK - 1):
        scale = work[:, j : j + 1] / work[j : j + 1, j : j + 1]
        work = work - jnp.where(row > j, scale * work[j : j + 1, :], 0.0)
    diagonal = jnp.sum(jnp.where(lane == row, work, 0.0), axis=1, keepdims=True)
    return work[:, RANK : 2 * RANK] / jnp.sqrt(diagonal)


def apply(inverse, block):
    total = inverse[:, 0:1] * block[0:1, :]
    for j in range(1, RANK):
        total = total + inverse[:, j : j + 1] * block[j : j + 1, :]
    return total


def by_column(low, high):
    tiles = [
        jnp.concatenate([low[4 * i : 4 * i + 4], high[4 * i : 4 * i + 4]], axis=0)
        for i in range(6)
    ]
    return jnp.concatenate(tiles[:5], axis=1), tiles[5]


def power(
    grad, error, q_init, q_out, p_out, m,
    gbuf, qv, cr, ra, rb, fm, fp, sx, s, s_high, s_low,
    p1s, p1r, qs, cbuf, zs, zbuf, qall, ps, pbuf, pfin, qfin,
    lsem, csend, crecv, ysend, yrecv, xsend, xrecv, p1sem, c1sem, zsem, c2sem, psem, fsem, qsend, qsame, qcross,
):
    d, t = lax.axis_index("dp"), lax.axis_index("tensor")
    y, c = d // 2, d % 2
    x, z = t // 8, t % 8

    def at(y_, c_, x_, z_):
        return (y_ * 2 + c_, x_ * 8 + z_)

    other = at(y, 1 - c, x, z)
    ahead_y, behind_y, far_y = (y + 1 + 2 * c) % 4, (y + 3 - 2 * c) % 4, (y + 2) % 4
    ahead, behind = at(ahead_y, c, x, z), at(behind_y, c, x, z)
    plane = [((y + j) % 4, (x + i) % 4) for i, j in PLANE]
    plane_same = [at(yy, c, xx, z) for yy, xx in plane]
    plane_other = [at(yy, 1 - c, xx, z) for yy, xx in plane]
    line = [at(y, c, x, (z + k) % 8) for k in (4, 3, 5, 2, 6, 1, 7)]

    def remote(src, dst, send, recv, device):
        copy = pltpu.make_async_remote_copy(
            src, dst, send, recv, device_id=device, device_id_type=MESH
        )
        copy.start()

    def wait(ref, sem):
        pltpu.make_async_copy(ref, ref, sem).wait()

    barrier = pltpu.get_barrier_semaphore()
    partners = line + plane_same + plane_other + [other]
    for device in partners:
        pl.semaphore_signal(barrier, inc=1, device_id=device, device_id_type=MESH)

    n = len(STARTS)
    loads = []
    for i, start in enumerate(STARTS):
        columns = pl.ds(start, min(CHUNK, COLS - start))
        loads.append((
            pltpu.make_async_copy(grad.at[0, :, columns], gbuf.at[:, columns], lsem.at[i]),
            pltpu.make_async_copy(error.at[0, :, columns], m.at[:, columns], lsem.at[n + i]),
        ))
        for copy in loads[-1]:
            copy.start()
    q_load = pltpu.make_async_copy(q_init, qv, lsem.at[2 * n])
    q_load.start()
    for i, start in enumerate(STARTS):
        for copy in loads[i]:
            copy.wait()
        columns = pl.ds(start, min(CHUNK, COLS - start))
        m[:, columns] = gbuf[:, columns].astype(F32) + m[:, columns]
    q_load.wait()
    pl.semaphore_wait(barrier, len(partners))

    def window(yy, xx):
        return pl.ds(pl.multiple_of(yy * STEP_Y + xx * WIN, LANE), WIN)

    mine = pl.ds(pl.multiple_of(HALF * c, 8), HALF)
    theirs = pl.ds(pl.multiple_of(HALF * (1 - c), 8), HALF)
    order = [(x + 1 + j) % 4 for j in range(4)]
    for xx in range(4):
        s[SLOT * xx + HALF : SLOT * (xx + 1), :] = jnp.zeros((SLOT - HALF, WIN), F32)
    turn = (far_y, ahead_y, behind_y, y)
    turn_there = (far_y, behind_y, ahead_y, y)
    for j in range(4):
        for k in range(4):
            yy = turn_there[k]
            remote(m.at[theirs, window(yy, order[j])], cr.at[order[j], yy], csend.at[j], crecv.at[k, j], other)

    top, low = pl.ds(0, TOP), pl.ds(TOP, HALF - TOP)

    def first(j):
        xx = order[j]

        def add(k):
            wait(cr.at[xx, turn[k]], crecv.at[k, j])
            cr[xx, turn[k]] = cr[xx, turn[k]] + m[mine, window(turn[k], xx)]

        add(0)
        remote(cr.at[xx, far_y, top], ra.at[j], ysend.at[0, j], yrecv.at[0, j], ahead)
        remote(cr.at[xx, far_y, low], rb.at[j], ysend.at[1, j], yrecv.at[1, j], behind)
        add(1)
        remote(cr.at[xx, ahead_y, low], fm.at[j, low], ysend.at[2, j], yrecv.at[2, j], ahead)
        add(2)
        remote(cr.at[xx, behind_y, top], fp.at[j, top], ysend.at[3, j], yrecv.at[3, j], behind)
        add(3)

    def second(j):
        xx = order[j]
        wait(ra.at[j], yrecv.at[0, j])
        ra[j] = ra[j] + cr[xx, ahead_y, top]
        remote(ra.at[j], fm.at[j, top], ysend.at[4, j], yrecv.at[4, j], ahead)
        wait(rb.at[j], yrecv.at[1, j])
        rb[j] = rb[j] + cr[xx, behind_y, low]
        remote(rb.at[j], fp.at[j, low], ysend.at[5, j], yrecv.at[5, j], behind)

    here = pl.ds(pl.multiple_of(SLOT * x, 8), HALF)

    def third(j):
        xx = order[j]
        wait(fm.at[j, low], yrecv.at[2, j])
        wait(fp.at[j, top], yrecv.at[3, j])
        wait(fm.at[j, top], yrecv.at[4, j])
        wait(fp.at[j, low], yrecv.at[5, j])
        total = (fm[j] + fp[j] + cr[xx, y]) * 0.125
        if j < 3:
            sx[j] = total
            remote(sx.at[j], s.at[here], xsend.at[0], xrecv.at[j], at(y, c, xx, z))
        else:
            s[here] = total

    first(0)
    first(1)

    q_two = stacked(qv[...])
    p_term = jnp.zeros((RANK, ROWS), F32)
    for start in STARTS:
        stop = min(start + CHUNK, COLS)
        high, rest = two_terms(m[:, start:stop])
        q_part = q_two[:, start:stop]
        on_high = nt(q_part, high.astype(BF16))
        on_rest = nt(q_part, rest.astype(BF16))
        p_term = p_term + (on_high[:RANK] + on_high[RANK:]) + (on_rest[:RANK] + on_rest[RANK:])
    blank = jnp.zeros((RANK, LANE - HALF), F32)
    for half in range(2):
        p1s[half] = jnp.concatenate([p_term[:, HALF * half : HALF * half + HALF], blank], axis=1)
    place = x * 8 + d
    p1r[place] = p1s[c]
    for same, cross in zip(plane_same, plane_other):
        remote(p1s.at[c], p1r.at[place], p1sem.at[0], p1sem.at[1], same)
        remote(p1s.at[1 - c], p1r.at[place], p1sem.at[0], p1sem.at[1], cross)
    remote(p1s.at[1 - c], p1r.at[place], p1sem.at[0], p1sem.at[1], other)

    second(0)
    first(2)
    second(1)
    third(0)
    second(2)
    first(3)
    third(1)

    wait(p1r.at[pl.ds(0, 31)], p1sem.at[1])
    blocks = []
    for xx in range(4):
        total = p1r[8 * xx]
        for dd in range(1, 8):
            total = total + p1r[8 * xx + dd]
        blocks.append(total[:, :SLOT])
    p_sum = jnp.concatenate(blocks, axis=1) * 0.125

    third(2)
    second(3)

    limit = jnp.where(jnp.logical_and(x == 3, y < 3), 3 * LANE, WIN)
    inside = lax.broadcasted_iota(jnp.int32, (SLOT, WIN), 1) < limit

    def terms(xx):
        rows = pl.ds(pl.multiple_of(SLOT * xx, SLOT), SLOT)
        high, rest = two_terms(jnp.where(inside, s[rows], 0.0))
        s_high[rows] = high.astype(BF16)
        s_low[rows] = rest.astype(BF16)

    for j in range(2):
        wait(sx.at[j], xrecv.at[j])
        terms((x + 3 - j) % 4)
    third(3)
    terms(x)
    wait(sx.at[2], xrecv.at[2])
    terms((x + 1) % 4)

    own = pl.ds(pl.multiple_of(PART * c, 8), PART)
    cross = pl.ds(pl.multiple_of(PART * (1 - c), 8), PART)
    pad = jnp.zeros((RANK, LANE - RANK), F32)
    me = y * 4 + x
    for i in range(ITERS):
        last = i == ITERS - 1
        p_two = stacked(p_sum)
        a, b = nn(p_two, s_high[...]), nn(p_two, s_low[...])
        q_raw = (a[:RANK] + a[RANK:]) + (b[:RANK] + b[RANK:])
        gram = lax.dot_general(
            p_sum, p_sum, (((1,), (1,)), ((), ())),
            precision=lax.Precision.HIGHEST, preferred_element_type=F32,
        )
        gram = jnp.concatenate([gram, pad], axis=1)
        for half in range(2):
            ranks = slice(4 * half, 4 * half + 4)
            for k in range(5):
                qs[i, PART * half + 4 * k : PART * half + 4 * k + 4, :] = q_raw[ranks, LANE * k : LANE * k + LANE]
            qs[i, PART * half + 20 : PART * half + 24, :] = gram[ranks]
        remote(qs.at[i, cross], cbuf.at[i], c1sem.at[0, i], c1sem.at[1, i], other)
        if last:
            rows = jnp.zeros((RANK, SLOT), F32)
            for xx in range(4):
                rows = jnp.where(x == xx, p_sum[:, SLOT * xx : SLOT * (xx + 1)], rows)
            pfin[c] = jnp.concatenate([rows, jnp.zeros((RANK, LANE - SLOT), F32)], axis=1)
            remote(pfin.at[c], pfin.at[c], fsem.at[0], fsem.at[1], other)
        wait(cbuf.at[i], c1sem.at[1, i])
        zs[i] = qs[i, own] + cbuf[i]
        zbuf[i, z] = zs[i]
        for device in line:
            remote(zs.at[i], zbuf.at[i, z], zsem.at[0, i], zsem.at[1, i], device)
        wait(zbuf.at[i, pl.ds(0, 7)], zsem.at[1, i])
        total = zbuf[i, 0]
        for k in range(1, 8):
            total = total + zbuf[i, k]
        if last:
            break
        qall[i, own] = total
        remote(qall.at[i, own], qall.at[i, own], c2sem.at[0, i], c2sem.at[1, i], other)
        wait(qall.at[i, own], c2sem.at[1, i])
        q_raw, gram = by_column(qall[i, 0:PART, :], qall[i, PART : 2 * PART, :])
        q_two = stacked(q_raw)
        a, b = nt(q_two, s_high[...]), nt(q_two, s_low[...])
        p_raw = (a[:RANK] + a[RANK:]) + (b[:RANK] + b[RANK:])
        ps[i, 0:RANK, :] = p_raw[:, :LANE]
        ps[i, RANK : 2 * RANK, :] = p_raw[:, LANE:]
        for device in plane_same:
            remote(ps.at[i], pbuf.at[i, me], psem.at[0, i], psem.at[1, i], device)
        pbuf[i, me] = ps[i]
        inverse = inverse_factor(gram)
        wait(pbuf.at[i, pl.ds(0, 15)], psem.at[1, i])
        p_raw = pbuf[i, 0]
        for k in range(1, 16):
            p_raw = p_raw + pbuf[i, k]
        p_raw = jnp.concatenate([p_raw[:RANK], p_raw[RANK:]], axis=1)
        p_sum = apply(inverse, p_raw)

    slot = me * 2 + c
    qfin[slot] = total
    remote(qfin.at[slot], qfin.at[slot], qsend.at[1], qcross.at[me], other)
    for device in plane_same:
        remote(qfin.at[slot], qfin.at[slot], qsend.at[0], qsame.at[me], device)
    wait(qfin.at[0], qcross.at[me])
    wait(pfin.at[c], fsem.at[1])
    _, gram = by_column(qfin[me * 2], qfin[me * 2 + 1])
    inverse = inverse_factor(gram)
    p_hat = apply(inverse, jnp.concatenate([pfin[0][:, :HALF], pfin[1][:, :HALF]], axis=1))
    p_out[...] = jnp.concatenate([p_hat, jnp.zeros((RANK, LANE - ROWS), F32)], axis=1)

    def result(yy, xx, arrived=False):
        group = yy * 4 + xx
        if not arrived:
            wait(qfin.at[0], qcross.at[group])
        q_raw, _ = by_column(qfin[group * 2], qfin[group * 2 + 1])
        q_sum = apply(inverse, q_raw)
        start = pl.multiple_of(yy * STEP_Y + xx * WIN, LANE)
        q_out[:, pl.ds(start, 3 * LANE)] = q_sum[:, : 3 * LANE]

        @pl.when(jnp.logical_or(xx < 3, yy == 3))
        def _():
            q_out[:, pl.ds(pl.multiple_of(start + 3 * LANE, LANE), 2 * LANE)] = q_sum[:, 3 * LANE :]

    result(y, x, True)
    nearest = plane[::-1]
    for k, (yy, xx) in enumerate(nearest):
        group = yy * 4 + xx
        wait(qfin.at[0], qsame.at[group])
        passed = qfin.at[group * 2 + c]
        remote(passed, passed, qsend.at[1], qcross.at[group], other)
        if k > 1:
            result(*nearest[k - 2])
    result(*nearest[-2])
    result(*nearest[-1])

    for j in range(4):
        wait(cr.at[j], csend.at[j])
        wait(ra.at[j], ysend.at[0, j])
        wait(rb.at[j], ysend.at[1, j])
        wait(fm.at[j, low], ysend.at[2, j])
        wait(fp.at[j, top], ysend.at[3, j])
        wait(ra.at[j], ysend.at[4, j])
        wait(rb.at[j], ysend.at[5, j])
    wait(sx, xsend.at[0])
    wait(p1r.at[pl.ds(0, 31)], p1sem.at[0])
    for i in range(ITERS):
        wait(cbuf.at[i], c1sem.at[0, i])
        wait(zbuf.at[i, pl.ds(0, 7)], zsem.at[0, i])
        if i < ITERS - 1:
            wait(cbuf.at[i], c2sem.at[0, i])
            wait(pbuf.at[i, pl.ds(0, 15)], psem.at[0, i])
    wait(pfin.at[0], fsem.at[0])
    wait(qfin.at[pl.ds(0, 15)], qsend.at[0])
    wait(qfin.at[pl.ds(0, 16)], qsend.at[1])


def factors(grad, error, q_init):
    dma = pltpu.SemaphoreType.DMA
    vmem = pltpu.VMEM
    return pl.pallas_call(
        power,
        name="factors",
        out_shape=(
            jax.ShapeDtypeStruct((RANK, COLS), F32),
            jax.ShapeDtypeStruct((RANK, LANE), F32),
            jax.ShapeDtypeStruct((ROWS, COLS), F32),
        ),
        in_specs=[pl.BlockSpec(memory_space=pltpu.HBM)] * 3,
        out_specs=(pl.BlockSpec(memory_space=vmem),) * 3,
        scratch_shapes=[
            vmem((ROWS, COLS), BF16),
            vmem((RANK, COLS), F32),
            vmem((4, 4, HALF, WIN), F32),
            vmem((4, TOP, WIN), F32),
            vmem((4, HALF - TOP, WIN), F32),
            vmem((4, HALF, WIN), F32),
            vmem((4, HALF, WIN), F32),
            vmem((3, HALF, WIN), F32),
            vmem((4 * SLOT, WIN), F32),
            vmem((4 * SLOT, WIN), BF16),
            vmem((4 * SLOT, WIN), BF16),
            vmem((2, RANK, LANE), F32),
            vmem((32, RANK, LANE), F32),
            vmem((ITERS, 2 * PART, LANE), F32),
            vmem((ITERS, PART, LANE), F32),
            vmem((ITERS, PART, LANE), F32),
            vmem((ITERS, 8, PART, LANE), F32),
            vmem((ITERS, 2 * PART, LANE), F32),
            vmem((ITERS, 2 * RANK, LANE), F32),
            vmem((ITERS, 16, 2 * RANK, LANE), F32),
            vmem((2, RANK, LANE), F32),
            vmem((32, PART, LANE), F32),
            dma((2 * len(STARTS) + 1,)),
            dma((4,)),
            dma((4, 4)),
            dma((6, 4)),
            dma((6, 4)),
            dma((1,)),
            dma((3,)),
            dma((2,)),
            dma((2, ITERS)),
            dma((2, ITERS)),
            dma((2, ITERS)),
            dma((2, ITERS)),
            dma((2,)),
            dma((2,)),
            dma((16,)),
            dma((16,)),
        ],
        compiler_params=pltpu.CompilerParams(
            collective_id=0, has_side_effects=True, vmem_limit_bytes=40 * 2**20
        ),
    )(*(pltpu.with_memory_space_constraint(a, pltpu.HBM) for a in (grad, error, q_init)))


def finish(p, q, m, decompressed, new_error, q_next, dbuf, ebuf, sem):
    copies = [pltpu.make_async_copy(q, q_next, sem.at[0])]
    copies[0].start()
    p_high, p_rest = two_terms(p[:, :ROWS])
    left = jnp.concatenate([p_high, p_high, p_rest, p_rest], axis=0).astype(BF16)
    for i, start in enumerate(STARTS):
        columns = pl.ds(start, min(CHUNK, COLS - start))
        q_high, q_rest = two_terms(q[:, columns])
        right = jnp.concatenate([q_high, q_rest, q_high, q_rest], axis=0).astype(BF16)
        approx = lax.dot_general(
            left, right, (((0,), (0,)), ((), ())), preferred_element_type=F32
        )
        ebuf[:, columns] = m[:, columns] - approx
        copies.append(pltpu.make_async_copy(ebuf.at[:, columns], new_error.at[0, :, columns], sem.at[2 * i + 1]))
        copies[-1].start()
        dbuf[:, columns] = approx.astype(BF16)
        copies.append(pltpu.make_async_copy(dbuf.at[:, columns], decompressed.at[:, columns], sem.at[2 * i + 2]))
        copies[-1].start()
    for copy in copies:
        copy.wait()


def outputs(p_hat, q_sum, merged):
    return pl.pallas_call(
        finish,
        name="outputs",
        in_specs=[pl.BlockSpec(memory_space=pltpu.VMEM)] * 3,
        out_specs=(pl.BlockSpec(memory_space=pltpu.HBM),) * 3,
        out_shape=(
            jax.ShapeDtypeStruct((ROWS, COLS), BF16),
            jax.ShapeDtypeStruct((1, ROWS, COLS), F32),
            jax.ShapeDtypeStruct((RANK, COLS), F32),
        ),
        scratch_shapes=[
            pltpu.VMEM((ROWS, COLS), BF16),
            pltpu.VMEM((ROWS, COLS), F32),
            pltpu.SemaphoreType.DMA((2 * len(STARTS) + 1,)),
        ],
        compiler_params=pltpu.CompilerParams(vmem_limit_bytes=24 * 2**20),
    )(p_hat, q_sum, merged)


def local(grad, error, q_init):
    q_sum, p_hat, merged = factors(grad, error, q_init)
    return outputs(p_hat, q_sum, merged)


def solution(mesh):
    return jax.shard_map(
        local,
        mesh=mesh,
        in_specs=(P("dp", "tensor", None), P("dp", "tensor", None), P()),
        out_specs=(P("tensor", None), P("dp", "tensor", None), P()),
        check_vma=False,
    )
```

```python
import jax
import jax.numpy as jnp
from jax import lax
from jax.experimental import pallas as pl
from jax.experimental.pallas import tpu as pltpu
from jax.sharding import PartitionSpec as P

MESH = pl.DeviceIdType.MESH
F32, BF16 = jnp.float32, jnp.bfloat16
ITERS = 4
RANK = 8
ROWS = 112
HALF = 56
SLOT = 64
COLS = 9472
LANE = 128
WIN = 640
TOP = 32
PART = 24
CHUNK = 10 * LANE
STARTS = tuple(range(0, COLS, CHUNK))
PLANE = sorted(
    ((i, j) for i in range(4) for j in range(4) if i or j),
    key=lambda ij: -(min(ij[0], 4 - ij[0]) + min(ij[1], 4 - ij[1])),
)


def first_tile(y, x):
    return 18 * y + y // 2 + 5 * x


def nt(a, b):
    return lax.dot_general(a, b, (((1,), (1,)), ((), ())), preferred_element_type=F32)


def nn(a, b):
    return lax.dot_general(a, b, (((1,), (0,)), ((), ())), preferred_element_type=F32)


def two_terms(a):
    high = a.astype(BF16).astype(F32)
    return high, a - high


def stacked(a):
    return jnp.concatenate(two_terms(a), axis=0).astype(BF16)


def inverse_factor(gram):
    shape = (RANK, LANE)
    row = lax.broadcasted_iota(jnp.int32, shape, 0)
    lane = lax.broadcasted_iota(jnp.int32, shape, 1)
    work = jnp.where(lane == row + RANK, 1.0, jnp.where(lane < RANK, gram, 0.0))
    for j in range(RANK - 1):
        scale = work[:, j : j + 1] / work[j : j + 1, j : j + 1]
        work = work - jnp.where(row > j, scale * work[j : j + 1, :], 0.0)
    diagonal = jnp.sum(jnp.where(lane == row, work, 0.0), axis=1, keepdims=True)
    return work[:, RANK : 2 * RANK] / jnp.sqrt(diagonal)


def apply(inverse, block):
    total = inverse[:, 0:1] * block[0:1, :]
    for j in range(1, RANK):
        total = total + inverse[:, j : j + 1] * block[j : j + 1, :]
    return total


def by_column(low, high):
    tiles = [
        jnp.concatenate([low[4 * i : 4 * i + 4], high[4 * i : 4 * i + 4]], axis=0)
        for i in range(6)
    ]
    return jnp.concatenate(tiles[:5], axis=1), tiles[5]


def power(
    grad, error, q_init, q_out, p_out, m,
    gbuf, qv, cr, ra, rb, fm, fp, sx, s, s_high, s_low,
    p1y, p1x, qs, cbuf, zs, zbuf, qall, ps, pbuf, pfin, qfin,
    lsem, csend, crecv, ysend, yrecv, xsend, xrecv, p1sem, c1sem, zsem, c2sem, psem, fsem, qsend, qsame, qcross,
):
    s[...] = jnp.zeros_like(s)
    d, t = lax.axis_index("dp"), lax.axis_index("tensor")
    y, c = d // 2, d % 2
    x, z = t // 8, t % 8

    def at(y_, c_, x_, z_):
        return (y_ * 2 + c_, x_ * 8 + z_)

    other = at(y, 1 - c, x, z)
    ahead_y, behind_y, far_y = (y + 1 + 2 * c) % 4, (y + 3 - 2 * c) % 4, (y + 2) % 4
    ahead, behind = at(ahead_y, c, x, z), at(behind_y, c, x, z)
    plane = [((y + j) % 4, (x + i) % 4) for i, j in PLANE]
    plane_same = [at(yy, c, xx, z) for yy, xx in plane]
    plane_other = [at(yy, 1 - c, xx, z) for yy, xx in plane]
    line = [at(y, c, x, (z + k) % 8) for k in (4, 3, 5, 2, 6, 1, 7)]

    def remote(src, dst, send, recv, device):
        copy = pltpu.make_async_remote_copy(
            src, dst, send, recv, device_id=device, device_id_type=MESH
        )
        copy.start()

    def wait(ref, sem):
        pltpu.make_async_copy(ref, ref, sem).wait()

    barrier = pltpu.get_barrier_semaphore()
    partners = line + plane_same + plane_other + [other]
    for device in partners:
        pl.semaphore_signal(barrier, inc=1, device_id=device, device_id_type=MESH)

    n = len(STARTS)
    loads = []
    for i, start in enumerate(STARTS):
        columns = pl.ds(start, min(CHUNK, COLS - start))
        loads.append((
            pltpu.make_async_copy(grad.at[0, :, columns], gbuf.at[:, columns], lsem.at[i]),
            pltpu.make_async_copy(error.at[0, :, columns], m.at[:, columns], lsem.at[n + i]),
        ))
        for copy in loads[-1]:
            copy.start()
    q_load = pltpu.make_async_copy(q_init, qv, lsem.at[2 * n])
    q_load.start()
    for i, start in enumerate(STARTS):
        for copy in loads[i]:
            copy.wait()
        columns = pl.ds(start, min(CHUNK, COLS - start))
        m[:, columns] = gbuf[:, columns].astype(F32) + m[:, columns]
    q_load.wait()
    pl.semaphore_wait(barrier, len(partners))

    def window(yy, xx, width):
        return pl.ds(pl.multiple_of(first_tile(yy, xx) * LANE, LANE), width)

    def sized(xx, body):
        @pl.when(xx < 3)
        def _():
            body(WIN)

        @pl.when(xx == 3)
        def _():
            body(WIN - LANE)

    mine = pl.ds(pl.multiple_of(HALF * c, 8), HALF)
    theirs = pl.ds(pl.multiple_of(HALF * (1 - c), 8), HALF)
    order = [(x + 1 + j) % 4 for j in range(4)]
    turn = (far_y, ahead_y, behind_y, y)
    turn_there = (far_y, behind_y, ahead_y, y)
    top, low = pl.ds(0, TOP), pl.ds(TOP, HALF - TOP)
    here = pl.ds(pl.multiple_of(SLOT * x, 8), HALF)

    def cross_core(j):
        def body(width):
            for k in range(4):
                yy = turn_there[k]
                remote(
                    m.at[theirs, window(yy, order[j], width)],
                    cr.at[order[j], yy, :, pl.ds(0, width)],
                    csend.at[j], crecv.at[k, j], other,
                )

        sized(order[j], body)

    def add(j, k, width):
        columns = pl.ds(0, width)
        place = cr.at[order[j], turn[k], :, columns]
        wait(place, crecv.at[k, j])
        place[...] = place[...] + m[mine, window(turn[k], order[j], width)]

    def first(j, added=False):
        def body(width):
            columns = pl.ds(0, width)
            xx = order[j]
            if not added:
                add(j, 0, width)
            remote(cr.at[xx, far_y, top, columns], ra.at[j, :, columns], ysend.at[0, j], yrecv.at[0, j], ahead)
            remote(cr.at[xx, far_y, low, columns], rb.at[j, :, columns], ysend.at[1, j], yrecv.at[1, j], behind)
            if not added:
                add(j, 1, width)
            remote(cr.at[xx, ahead_y, low, columns], fm.at[j, low, columns], ysend.at[2, j], yrecv.at[2, j], ahead)
            if not added:
                add(j, 2, width)
            remote(cr.at[xx, behind_y, top, columns], fp.at[j, top, columns], ysend.at[3, j], yrecv.at[3, j], behind)
            if not added:
                add(j, 3, width)

        sized(order[j], body)

    def only_add(j):
        def body(width):
            for k in range(4):
                add(j, k, width)

        sized(order[j], body)

    def second(j):
        def body(width):
            columns = pl.ds(0, width)
            xx = order[j]
            a, b = ra.at[j, :, columns], rb.at[j, :, columns]
            wait(a, yrecv.at[0, j])
            a[...] = a[...] + cr[xx, ahead_y, top, columns]
            remote(a, fm.at[j, top, columns], ysend.at[4, j], yrecv.at[4, j], ahead)
            wait(b, yrecv.at[1, j])
            b[...] = b[...] + cr[xx, behind_y, low, columns]
            remote(b, fp.at[j, low, columns], ysend.at[5, j], yrecv.at[5, j], behind)

        sized(order[j], body)

    def third(j):
        def body(width):
            columns = pl.ds(0, width)
            xx = order[j]
            wait(fm.at[j, low, columns], yrecv.at[2, j])
            wait(fp.at[j, top, columns], yrecv.at[3, j])
            wait(fm.at[j, top, columns], yrecv.at[4, j])
            wait(fp.at[j, low, columns], yrecv.at[5, j])
            total = (fm[j, :, columns] + fp[j, :, columns] + cr[xx, y, :, columns]) * 0.125
            if j < 3:
                sx[j, :, columns] = total
                remote(sx.at[j, :, columns], s.at[here, columns], xsend.at[j], xrecv.at[j], at(y, c, xx, z))
            else:
                s[here, columns] = total

        sized(order[j], body)

    for j in range(4):
        cross_core(j)
    first(0)
    first(1)
    first(2)
    only_add(3)

    q_two = stacked(qv[...])
    p_term = jnp.zeros((RANK, HALF), F32)
    for yy in range(4):
        for xx in range(4):
            start = first_tile(yy, xx) * LANE
            width = (5 if xx < 3 else 3 + yy % 2) * LANE
            high, rest = two_terms(cr[xx, yy, :, :width])
            q_part = q_two[:, start : start + width]
            on_high = nt(q_part, high.astype(BF16))
            on_rest = nt(q_part, rest.astype(BF16))
            p_term = p_term + (on_high[:RANK] + on_high[RANK:]) + (on_rest[:RANK] + on_rest[RANK:])
    p1y[y] = jnp.concatenate([p_term, jnp.zeros((RANK, LANE - HALF), F32)], axis=1)
    for k in (2, 1, 3):
        remote(p1y.at[y], p1y.at[y], p1sem.at[0], p1sem.at[1], at((y + k) % 4, c, x, z))

    second(0)
    second(1)
    wait(p1y.at[pl.ds(0, 3)], p1sem.at[1])
    p1x[x] = ((p1y[0] + p1y[1]) + (p1y[2] + p1y[3])) * 0.125
    for k in (2, 1, 3):
        remote(p1x.at[x], p1x.at[x], p1sem.at[2], p1sem.at[3], at(y, c, (x + k) % 4, z))
    third(0)
    second(2)
    first(3, True)
    third(1)
    wait(p1x.at[pl.ds(0, 3)], p1sem.at[3])
    p_sum = jnp.concatenate([p1x[xx][:, :SLOT] for xx in range(4)], axis=1)
    third(2)
    second(3)

    limit = jnp.where(x == 3, (3 + y % 2) * LANE, WIN)
    inside = lax.broadcasted_iota(jnp.int32, (SLOT, WIN), 1) < limit

    def terms(xx):
        rows = pl.ds(pl.multiple_of(SLOT * xx, SLOT), SLOT)
        high, rest = two_terms(jnp.where(inside, s[rows], 0.0))
        s_high[rows] = high.astype(BF16)
        s_low[rows] = rest.astype(BF16)

    def from_x(j):
        sized(x, lambda width: wait(sx.at[j, :, pl.ds(0, width)], xrecv.at[j]))
        terms((x + 3 - j) % 4)

    from_x(0)
    from_x(1)
    third(3)
    terms(x)
    from_x(2)

    own = pl.ds(pl.multiple_of(PART * c, 8), PART)
    cross = pl.ds(pl.multiple_of(PART * (1 - c), 8), PART)
    pad = jnp.zeros((RANK, LANE - RANK), F32)
    me = y * 4 + x
    for i in range(ITERS):
        last = i == ITERS - 1
        p_two = stacked(p_sum)
        a, b = nn(p_two, s_high[...]), nn(p_two, s_low[...])
        q_raw = (a[:RANK] + a[RANK:]) + (b[:RANK] + b[RANK:])
        gram = lax.dot_general(
            p_sum, p_sum, (((1,), (1,)), ((), ())),
            precision=lax.Precision.HIGHEST, preferred_element_type=F32,
        )
        gram = jnp.concatenate([gram, pad], axis=1)
        for half in range(2):
            ranks = slice(4 * half, 4 * half + 4)
            for k in range(5):
                qs[i, PART * half + 4 * k : PART * half + 4 * k + 4, :] = q_raw[ranks, LANE * k : LANE * k + LANE]
            qs[i, PART * half + 20 : PART * half + 24, :] = gram[ranks]
        remote(qs.at[i, cross], cbuf.at[i], c1sem.at[0, i], c1sem.at[1, i], other)
        if last:
            rows = jnp.zeros((RANK, SLOT), F32)
            for xx in range(4):
                rows = jnp.where(x == xx, p_sum[:, SLOT * xx : SLOT * (xx + 1)], rows)
            pfin[c] = jnp.concatenate([rows, jnp.zeros((RANK, LANE - SLOT), F32)], axis=1)
            remote(pfin.at[c], pfin.at[c], fsem.at[0], fsem.at[1], other)
        wait(cbuf.at[i], c1sem.at[1, i])
        zs[i] = qs[i, own] + cbuf[i]
        zbuf[i, z] = zs[i]
        for device in line:
            remote(zs.at[i], zbuf.at[i, z], zsem.at[0, i], zsem.at[1, i], device)
        wait(zbuf.at[i, pl.ds(0, 7)], zsem.at[1, i])
        total = zbuf[i, 0]
        for k in range(1, 8):
            total = total + zbuf[i, k]
        if last:
            break
        qall[i, own] = total
        remote(qall.at[i, own], qall.at[i, own], c2sem.at[0, i], c2sem.at[1, i], other)
        wait(qall.at[i, own], c2sem.at[1, i])
        q_raw, gram = by_column(qall[i, 0:PART, :], qall[i, PART : 2 * PART, :])
        q_two = stacked(q_raw)
        a, b = nt(q_two, s_high[...]), nt(q_two, s_low[...])
        p_raw = (a[:RANK] + a[RANK:]) + (b[:RANK] + b[RANK:])
        ps[i, 0:RANK, :] = p_raw[:, :LANE]
        ps[i, RANK : 2 * RANK, :] = p_raw[:, LANE:]
        for device in plane_same:
            remote(ps.at[i], pbuf.at[i, me], psem.at[0, i], psem.at[1, i], device)
        pbuf[i, me] = ps[i]
        inverse = inverse_factor(gram)
        wait(pbuf.at[i, pl.ds(0, 15)], psem.at[1, i])
        p_raw = pbuf[i, 0]
        for k in range(1, 16):
            p_raw = p_raw + pbuf[i, k]
        p_raw = jnp.concatenate([p_raw[:RANK], p_raw[RANK:]], axis=1)
        p_sum = apply(inverse, p_raw)

    slot = me * 2 + c
    qfin[slot] = total
    remote(qfin.at[slot], qfin.at[slot], qsend.at[1], qcross.at[me], other)
    for device in plane_same:
        remote(qfin.at[slot], qfin.at[slot], qsend.at[0], qsame.at[me], device)
    wait(qfin.at[0], qcross.at[me])
    wait(pfin.at[c], fsem.at[1])
    _, gram = by_column(qfin[me * 2], qfin[me * 2 + 1])
    inverse = inverse_factor(gram)
    p_hat = apply(inverse, jnp.concatenate([pfin[0][:, :HALF], pfin[1][:, :HALF]], axis=1))
    p_out[...] = jnp.concatenate([p_hat, jnp.zeros((RANK, LANE - ROWS), F32)], axis=1)

    nearest = plane[::-1]
    for yy, xx in nearest:
        group = yy * 4 + xx
        wait(qfin.at[0], qsame.at[group])
        passed = qfin.at[group * 2 + c]
        remote(passed, passed, qsend.at[1], qcross.at[group], other)
    by_rank = [jnp.broadcast_to(inverse[:, j : j + 1], (RANK, LANE)) for j in range(RANK)]
    for yy, xx in nearest:
        wait(qfin.at[0], qcross.at[yy * 4 + xx])
    for yy in range(4):
        for xx in range(4):
            group, start = yy * 4 + xx, first_tile(yy, xx)
            for k in range(5 if xx < 3 else 3 + yy % 2):
                terms_of = [
                    by_rank[j] * qfin[2 * group + j // 4, 4 * k + j % 4 : 4 * k + j % 4 + 1, :]
                    for j in range(RANK)
                ]
                tile = ((terms_of[0] + terms_of[1]) + (terms_of[2] + terms_of[3])) + (
                    (terms_of[4] + terms_of[5]) + (terms_of[6] + terms_of[7])
                )
                q_out[:, LANE * (start + k) : LANE * (start + k + 1)] = tile

    def left(j):
        def body(width):
            columns = pl.ds(0, width)
            wait(cr.at[order[j], :, :, columns], csend.at[j])
            wait(ra.at[j, :, columns], ysend.at[0, j])
            wait(rb.at[j, :, columns], ysend.at[1, j])
            wait(fm.at[j, low, columns], ysend.at[2, j])
            wait(fp.at[j, top, columns], ysend.at[3, j])
            wait(ra.at[j, :, columns], ysend.at[4, j])
            wait(rb.at[j, :, columns], ysend.at[5, j])
            if j < 3:
                wait(sx.at[j, :, columns], xsend.at[j])

        sized(order[j], body)

    for j in range(4):
        left(j)
    wait(p1y.at[pl.ds(0, 3)], p1sem.at[0])
    wait(p1x.at[pl.ds(0, 3)], p1sem.at[2])
    for i in range(ITERS):
        wait(cbuf.at[i], c1sem.at[0, i])
        wait(zbuf.at[i, pl.ds(0, 7)], zsem.at[0, i])
        if i < ITERS - 1:
            wait(cbuf.at[i], c2sem.at[0, i])
            wait(pbuf.at[i, pl.ds(0, 15)], psem.at[0, i])
    wait(pfin.at[0], fsem.at[0])
    wait(qfin.at[pl.ds(0, 15)], qsend.at[0])
    wait(qfin.at[pl.ds(0, 16)], qsend.at[1])


def factors(grad, error, q_init):
    dma = pltpu.SemaphoreType.DMA
    vmem = pltpu.VMEM
    return pl.pallas_call(
        power,
        name="factors",
        out_shape=(
            jax.ShapeDtypeStruct((RANK, COLS), F32),
            jax.ShapeDtypeStruct((RANK, LANE), F32),
            jax.ShapeDtypeStruct((ROWS, COLS), F32),
        ),
        in_specs=[pl.BlockSpec(memory_space=pltpu.HBM)] * 3,
        out_specs=(pl.BlockSpec(memory_space=vmem),) * 3,
        scratch_shapes=[
            vmem((ROWS, COLS), BF16),
            vmem((RANK, COLS), F32),
            vmem((4, 4, HALF, WIN), F32),
            vmem((4, TOP, WIN), F32),
            vmem((4, HALF - TOP, WIN), F32),
            vmem((4, HALF, WIN), F32),
            vmem((4, HALF, WIN), F32),
            vmem((3, HALF, WIN), F32),
            vmem((4 * SLOT, WIN), F32),
            vmem((4 * SLOT, WIN), BF16),
            vmem((4 * SLOT, WIN), BF16),
            vmem((4, RANK, LANE), F32),
            vmem((4, RANK, LANE), F32),
            vmem((ITERS, 2 * PART, LANE), F32),
            vmem((ITERS, PART, LANE), F32),
            vmem((ITERS, PART, LANE), F32),
            vmem((ITERS, 8, PART, LANE), F32),
            vmem((ITERS, 2 * PART, LANE), F32),
            vmem((ITERS, 2 * RANK, LANE), F32),
            vmem((ITERS, 16, 2 * RANK, LANE), F32),
            vmem((2, RANK, LANE), F32),
            vmem((32, PART, LANE), F32),
            dma((2 * len(STARTS) + 1,)),
            dma((4,)),
            dma((4, 4)),
            dma((6, 4)),
            dma((6, 4)),
            dma((3,)),
            dma((3,)),
            dma((4,)),
            dma((2, ITERS)),
            dma((2, ITERS)),
            dma((2, ITERS)),
            dma((2, ITERS)),
            dma((2,)),
            dma((2,)),
            dma((16,)),
            dma((16,)),
        ],
        compiler_params=pltpu.CompilerParams(
            collective_id=0, has_side_effects=True, vmem_limit_bytes=40 * 2**20
        ),
    )(*(pltpu.with_memory_space_constraint(a, pltpu.HBM) for a in (grad, error, q_init)))


PARTS = (2, 4, 8, 10, 10, 10, 10, 10, 6, 4)


def finish(p, q, m, decompressed, new_error, q_next, dbuf, ebuf, sem):
    copies = [pltpu.make_async_copy(q, q_next, sem.at[0])]
    copies[0].start()
    p_high, p_rest = two_terms(p[:, :ROWS])
    left = jnp.concatenate([p_high, p_high, p_rest, p_rest], axis=0).astype(BF16)
    start = 0
    for i, part in enumerate(PARTS):
        columns = pl.ds(start, part * LANE)
        start += part * LANE
        q_high, q_rest = two_terms(q[:, columns])
        right = jnp.concatenate([q_high, q_rest, q_high, q_rest], axis=0).astype(BF16)
        approx = lax.dot_general(
            left, right, (((0,), (0,)), ((), ())), preferred_element_type=F32
        )
        ebuf[:, columns] = m[:, columns] - approx
        copies.append(pltpu.make_async_copy(ebuf.at[:, columns], new_error.at[0, :, columns], sem.at[2 * i + 1]))
        copies[-1].start()
        dbuf[:, columns] = approx.astype(BF16)
        copies.append(pltpu.make_async_copy(dbuf.at[:, columns], decompressed.at[:, columns], sem.at[2 * i + 2]))
        copies[-1].start()
    for copy in copies:
        copy.wait()


def outputs(p_hat, q_sum, merged):
    return pl.pallas_call(
        finish,
        name="outputs",
        in_specs=[pl.BlockSpec(memory_space=pltpu.VMEM)] * 3,
        out_specs=(pl.BlockSpec(memory_space=pltpu.HBM),) * 3,
        out_shape=(
            jax.ShapeDtypeStruct((ROWS, COLS), BF16),
            jax.ShapeDtypeStruct((1, ROWS, COLS), F32),
            jax.ShapeDtypeStruct((RANK, COLS), F32),
        ),
        scratch_shapes=[
            pltpu.VMEM((ROWS, COLS), BF16),
            pltpu.VMEM((ROWS, COLS), F32),
            pltpu.SemaphoreType.DMA((2 * len(PARTS) + 1,)),
        ],
        compiler_params=pltpu.CompilerParams(vmem_limit_bytes=24 * 2**20),
    )(p_hat, q_sum, merged)


def local(grad, error, q_init):
    q_sum, p_hat, merged = factors(grad, error, q_init)
    return outputs(p_hat, q_sum, merged)


def solution(mesh):
    return jax.shard_map(
        local,
        mesh=mesh,
        in_specs=(P("dp", "tensor", None), P("dp", "tensor", None), P()),
        out_specs=(P("tensor", None), P("dp", "tensor", None), P()),
        check_vma=False,
    )
```

```python
import jax
import jax.numpy as jnp
from jax import lax
from jax.experimental import pallas as pl
from jax.experimental.pallas import tpu as pltpu
from jax.sharding import PartitionSpec as P

MESH = pl.DeviceIdType.MESH
F32, BF16 = jnp.float32, jnp.bfloat16
ITERS = 4
RANK = 8
ROWS = 112
HALF = 56
SLOT = 64
COLS = 9472
LANE = 128
WIN = 640
TOP = 32
PART = 24
CHUNK = 10 * LANE
STARTS = tuple(range(0, COLS, CHUNK))
PLANE = sorted(
    ((i, j) for i in range(4) for j in range(4) if i or j),
    key=lambda ij: -(min(ij[0], 4 - ij[0]) + min(ij[1], 4 - ij[1])),
)


def first_tile(y, x):
    return 18 * y + y // 2 + 5 * x


def nt(a, b):
    return lax.dot_general(a, b, (((1,), (1,)), ((), ())), preferred_element_type=F32)


def nn(a, b):
    return lax.dot_general(a, b, (((1,), (0,)), ((), ())), preferred_element_type=F32)


def two_terms(a):
    high = a.astype(BF16).astype(F32)
    return high, a - high


def stacked(a):
    return jnp.concatenate(two_terms(a), axis=0).astype(BF16)


def inverse_factor(gram):
    shape = (RANK, LANE)
    row = lax.broadcasted_iota(jnp.int32, shape, 0)
    lane = lax.broadcasted_iota(jnp.int32, shape, 1)
    work = jnp.where(lane == row + RANK, 1.0, jnp.where(lane < RANK, gram, 0.0))
    for j in range(RANK - 1):
        scale = work[:, j : j + 1] / work[j : j + 1, j : j + 1]
        work = work - jnp.where(row > j, scale * work[j : j + 1, :], 0.0)
    diagonal = jnp.sum(jnp.where(lane == row, work, 0.0), axis=1, keepdims=True)
    return work[:, RANK : 2 * RANK] / jnp.sqrt(diagonal)


def apply(inverse, block):
    total = inverse[:, 0:1] * block[0:1, :]
    for j in range(1, RANK):
        total = total + inverse[:, j : j + 1] * block[j : j + 1, :]
    return total


def by_column(low, high):
    tiles = [
        jnp.concatenate([low[4 * i : 4 * i + 4], high[4 * i : 4 * i + 4]], axis=0)
        for i in range(6)
    ]
    return jnp.concatenate(tiles[:5], axis=1), tiles[5]


def power(
    grad, error, q_init, q_out, p_out, m,
    gbuf, qv, cr, ra, rb, fm, fp, sx, s, s_high, s_low,
    p1y, p1x, qs, cbuf, zs, zbuf, qall, ps, pbuf, pfin, qfin,
    lsem, csend, crecv, ysend, yrecv, xsend, xrecv, p1sem, c1sem, zsem, c2sem, psem, fsem, qsend, qsame, qcross,
):
    s[...] = jnp.zeros_like(s)
    d, t = lax.axis_index("dp"), lax.axis_index("tensor")
    y, c = d // 2, d % 2
    x, z = t // 8, t % 8

    def at(y_, c_, x_, z_):
        return (y_ * 2 + c_, x_ * 8 + z_)

    other = at(y, 1 - c, x, z)
    ahead_y, behind_y, far_y = (y + 1 + 2 * c) % 4, (y + 3 - 2 * c) % 4, (y + 2) % 4
    ahead, behind = at(ahead_y, c, x, z), at(behind_y, c, x, z)
    plane = [((y + j) % 4, (x + i) % 4) for i, j in PLANE]
    plane_same = [at(yy, c, xx, z) for yy, xx in plane]
    line = [at(y, c, x, (z + k) % 8) for k in (4, 3, 5, 2, 6, 1, 7)]

    def remote(src, dst, send, recv, device):
        copy = pltpu.make_async_remote_copy(
            src, dst, send, recv, device_id=device, device_id_type=MESH
        )
        copy.start()

    def wait(ref, sem):
        pltpu.make_async_copy(ref, ref, sem).wait()

    barrier = pltpu.get_barrier_semaphore()
    partners = line + plane_same + [other]
    for device in partners:
        pl.semaphore_signal(barrier, inc=1, device_id=device, device_id_type=MESH)

    n = len(STARTS)
    loads = []
    for i, start in enumerate(STARTS):
        columns = pl.ds(start, min(CHUNK, COLS - start))
        loads.append((
            pltpu.make_async_copy(grad.at[0, :, columns], gbuf.at[:, columns], lsem.at[i]),
            pltpu.make_async_copy(error.at[0, :, columns], m.at[:, columns], lsem.at[n + i]),
        ))
        for copy in loads[-1]:
            copy.start()
    q_load = pltpu.make_async_copy(q_init, qv, lsem.at[2 * n])
    q_load.start()
    for i, start in enumerate(STARTS):
        for copy in loads[i]:
            copy.wait()
        columns = pl.ds(start, min(CHUNK, COLS - start))
        m[:, columns] = gbuf[:, columns].astype(F32) + m[:, columns]
    q_load.wait()
    pl.semaphore_wait(barrier, len(partners))

    def window(yy, xx, width):
        return pl.ds(pl.multiple_of(first_tile(yy, xx) * LANE, LANE), width)

    def sized(xx, body):
        @pl.when(xx < 3)
        def _():
            body(WIN)

        @pl.when(xx == 3)
        def _():
            body(WIN - LANE)

    mine = pl.ds(pl.multiple_of(HALF * c, 8), HALF)
    theirs = pl.ds(pl.multiple_of(HALF * (1 - c), 8), HALF)
    order = [(x + 1 + j) % 4 for j in range(4)]
    turn = (far_y, ahead_y, behind_y, y)
    turn_there = (far_y, behind_y, ahead_y, y)
    top, low = pl.ds(0, TOP), pl.ds(TOP, HALF - TOP)
    here = pl.ds(pl.multiple_of(SLOT * x, 8), HALF)

    def cross_core(j):
        def body(width):
            for k in range(4):
                yy = turn_there[k]
                remote(
                    m.at[theirs, window(yy, order[j], width)],
                    cr.at[order[j], yy, :, pl.ds(0, width)],
                    csend.at[j], crecv.at[k, j], other,
                )

        sized(order[j], body)

    def add(j, k, width):
        columns = pl.ds(0, width)
        place = cr.at[order[j], turn[k], :, columns]
        wait(place, crecv.at[k, j])
        place[...] = place[...] + m[mine, window(turn[k], order[j], width)]

    def first(j, added=False):
        def body(width):
            columns = pl.ds(0, width)
            xx = order[j]
            if not added:
                add(j, 0, width)
            remote(cr.at[xx, far_y, top, columns], ra.at[j, :, columns], ysend.at[0, j], yrecv.at[0, j], ahead)
            remote(cr.at[xx, far_y, low, columns], rb.at[j, :, columns], ysend.at[1, j], yrecv.at[1, j], behind)
            if not added:
                add(j, 1, width)
            remote(cr.at[xx, ahead_y, low, columns], fm.at[j, low, columns], ysend.at[2, j], yrecv.at[2, j], ahead)
            if not added:
                add(j, 2, width)
            remote(cr.at[xx, behind_y, top, columns], fp.at[j, top, columns], ysend.at[3, j], yrecv.at[3, j], behind)
            if not added:
                add(j, 3, width)

        sized(order[j], body)

    def only_add(j):
        def body(width):
            for k in range(4):
                add(j, k, width)

        sized(order[j], body)

    def second(j):
        def body(width):
            columns = pl.ds(0, width)
            xx = order[j]
            a, b = ra.at[j, :, columns], rb.at[j, :, columns]
            wait(a, yrecv.at[0, j])
            a[...] = a[...] + cr[xx, ahead_y, top, columns]
            remote(a, fm.at[j, top, columns], ysend.at[4, j], yrecv.at[4, j], ahead)
            wait(b, yrecv.at[1, j])
            b[...] = b[...] + cr[xx, behind_y, low, columns]
            remote(b, fp.at[j, low, columns], ysend.at[5, j], yrecv.at[5, j], behind)

        sized(order[j], body)

    def third(j):
        def body(width):
            columns = pl.ds(0, width)
            xx = order[j]
            wait(fm.at[j, low, columns], yrecv.at[2, j])
            wait(fp.at[j, top, columns], yrecv.at[3, j])
            wait(fm.at[j, top, columns], yrecv.at[4, j])
            wait(fp.at[j, low, columns], yrecv.at[5, j])
            total = (fm[j, :, columns] + fp[j, :, columns] + cr[xx, y, :, columns]) * 0.125
            if j < 3:
                sx[j, :, columns] = total
                remote(sx.at[j, :, columns], s.at[here, columns], xsend.at[j], xrecv.at[j], at(y, c, xx, z))
            else:
                s[here, columns] = total

        sized(order[j], body)

    for j in range(4):
        cross_core(j)
    first(0)
    first(1)
    first(2)
    only_add(3)

    q_two = stacked(qv[...])
    p_term = jnp.zeros((RANK, HALF), F32)
    for yy in range(4):
        for xx in range(4):
            start = first_tile(yy, xx) * LANE
            width = (5 if xx < 3 else 3 + yy % 2) * LANE
            high, rest = two_terms(cr[xx, yy, :, :width])
            q_part = q_two[:, start : start + width]
            on_high = nt(q_part, high.astype(BF16))
            on_rest = nt(q_part, rest.astype(BF16))
            p_term = p_term + (on_high[:RANK] + on_high[RANK:]) + (on_rest[:RANK] + on_rest[RANK:])
    p1y[y] = jnp.concatenate([p_term, jnp.zeros((RANK, LANE - HALF), F32)], axis=1)
    for k in (2, 1, 3):
        remote(p1y.at[y], p1y.at[y], p1sem.at[0], p1sem.at[1], at((y + k) % 4, c, x, z))

    second(0)
    second(1)
    wait(p1y.at[pl.ds(0, 3)], p1sem.at[1])
    p1x[x] = ((p1y[0] + p1y[1]) + (p1y[2] + p1y[3])) * 0.125
    for k in (2, 1, 3):
        remote(p1x.at[x], p1x.at[x], p1sem.at[2], p1sem.at[3], at(y, c, (x + k) % 4, z))
    third(0)
    second(2)
    first(3, True)
    third(1)
    wait(p1x.at[pl.ds(0, 3)], p1sem.at[3])
    p_sum = jnp.concatenate([p1x[xx][:, :SLOT] for xx in range(4)], axis=1)
    third(2)
    second(3)

    limit = jnp.where(x == 3, (3 + y % 2) * LANE, WIN)
    inside = lax.broadcasted_iota(jnp.int32, (SLOT, WIN), 1) < limit

    def terms(xx):
        rows = pl.ds(pl.multiple_of(SLOT * xx, SLOT), SLOT)
        high, rest = two_terms(jnp.where(inside, s[rows], 0.0))
        s_high[rows] = high.astype(BF16)
        s_low[rows] = rest.astype(BF16)

    def from_x(j):
        sized(x, lambda width: wait(sx.at[j, :, pl.ds(0, width)], xrecv.at[j]))
        terms((x + 3 - j) % 4)

    from_x(0)
    from_x(1)
    third(3)
    terms(x)
    from_x(2)

    own = pl.ds(pl.multiple_of(PART * c, 8), PART)
    cross = pl.ds(pl.multiple_of(PART * (1 - c), 8), PART)
    pad = jnp.zeros((RANK, LANE - RANK), F32)
    me = y * 4 + x
    for i in range(ITERS):
        last = i == ITERS - 1
        p_two = stacked(p_sum)
        a, b = nn(p_two, s_high[...]), nn(p_two, s_low[...])
        q_raw = (a[:RANK] + a[RANK:]) + (b[:RANK] + b[RANK:])
        gram = lax.dot_general(
            p_sum, p_sum, (((1,), (1,)), ((), ())),
            precision=lax.Precision.HIGHEST, preferred_element_type=F32,
        )
        gram = jnp.concatenate([gram, pad], axis=1)
        for half in range(2):
            ranks = slice(4 * half, 4 * half + 4)
            for k in range(5):
                qs[i, PART * half + 4 * k : PART * half + 4 * k + 4, :] = q_raw[ranks, LANE * k : LANE * k + LANE]
            qs[i, PART * half + 20 : PART * half + 24, :] = gram[ranks]
        remote(qs.at[i, cross], cbuf.at[i], c1sem.at[0, i], c1sem.at[1, i], other)
        if last:
            rows = jnp.zeros((RANK, SLOT), F32)
            for xx in range(4):
                rows = jnp.where(x == xx, p_sum[:, SLOT * xx : SLOT * (xx + 1)], rows)
            pfin[c] = jnp.concatenate([rows, jnp.zeros((RANK, LANE - SLOT), F32)], axis=1)
            remote(pfin.at[c], pfin.at[c], fsem.at[0], fsem.at[1], other)
        wait(cbuf.at[i], c1sem.at[1, i])
        zs[i] = qs[i, own] + cbuf[i]
        zbuf[i, z] = zs[i]
        for device in line:
            remote(zs.at[i], zbuf.at[i, z], zsem.at[0, i], zsem.at[1, i], device)
        wait(zbuf.at[i, pl.ds(0, 7)], zsem.at[1, i])
        total = zbuf[i, 0]
        for k in range(1, 8):
            total = total + zbuf[i, k]
        if last:
            break
        qall[i, own] = total
        remote(qall.at[i, own], qall.at[i, own], c2sem.at[0, i], c2sem.at[1, i], other)
        wait(qall.at[i, own], c2sem.at[1, i])
        q_raw, gram = by_column(qall[i, 0:PART, :], qall[i, PART : 2 * PART, :])
        q_two = stacked(q_raw)
        a, b = nt(q_two, s_high[...]), nt(q_two, s_low[...])
        p_raw = (a[:RANK] + a[RANK:]) + (b[:RANK] + b[RANK:])
        ps[i, 0:RANK, :] = p_raw[:, :LANE]
        ps[i, RANK : 2 * RANK, :] = p_raw[:, LANE:]
        for device in plane_same:
            remote(ps.at[i], pbuf.at[i, me], psem.at[0, i], psem.at[1, i], device)
        pbuf[i, me] = ps[i]
        inverse = inverse_factor(gram)
        wait(pbuf.at[i, pl.ds(0, 15)], psem.at[1, i])
        p_raw = pbuf[i, 0]
        for k in range(1, 16):
            p_raw = p_raw + pbuf[i, k]
        p_raw = jnp.concatenate([p_raw[:RANK], p_raw[RANK:]], axis=1)
        p_sum = apply(inverse, p_raw)

    slot = me * 2 + c
    qfin[slot] = total
    remote(qfin.at[slot], qfin.at[slot], qsend.at[1], qcross.at[me], other)
    for device in plane_same:
        remote(qfin.at[slot], qfin.at[slot], qsend.at[0], qsame.at[me], device)
    wait(qfin.at[0], qcross.at[me])
    wait(pfin.at[c], fsem.at[1])
    _, gram = by_column(qfin[me * 2], qfin[me * 2 + 1])
    inverse = inverse_factor(gram)
    p_hat = apply(inverse, jnp.concatenate([pfin[0][:, :HALF], pfin[1][:, :HALF]], axis=1))
    p_out[...] = jnp.concatenate([p_hat, jnp.zeros((RANK, LANE - ROWS), F32)], axis=1)

    nearest = plane[::-1]
    for yy, xx in nearest:
        group = yy * 4 + xx
        wait(qfin.at[0], qsame.at[group])
        passed = qfin.at[group * 2 + c]
        remote(passed, passed, qsend.at[1], qcross.at[group], other)
    by_rank = [jnp.broadcast_to(inverse[:, j : j + 1], (RANK, LANE)) for j in range(RANK)]
    for yy, xx in nearest:
        wait(qfin.at[0], qcross.at[yy * 4 + xx])
    for yy in range(4):
        for xx in range(4):
            group, start = yy * 4 + xx, first_tile(yy, xx)
            for k in range(5 if xx < 3 else 3 + yy % 2):
                terms_of = [
                    by_rank[j] * qfin[2 * group + j // 4, 4 * k + j % 4 : 4 * k + j % 4 + 1, :]
                    for j in range(RANK)
                ]
                tile = ((terms_of[0] + terms_of[1]) + (terms_of[2] + terms_of[3])) + (
                    (terms_of[4] + terms_of[5]) + (terms_of[6] + terms_of[7])
                )
                q_out[:, LANE * (start + k) : LANE * (start + k + 1)] = tile

    def left(j):
        def body(width):
            columns = pl.ds(0, width)
            wait(cr.at[order[j], :, :, columns], csend.at[j])
            wait(ra.at[j, :, columns], ysend.at[0, j])
            wait(rb.at[j, :, columns], ysend.at[1, j])
            wait(fm.at[j, low, columns], ysend.at[2, j])
            wait(fp.at[j, top, columns], ysend.at[3, j])
            wait(ra.at[j, :, columns], ysend.at[4, j])
            wait(rb.at[j, :, columns], ysend.at[5, j])
            if j < 3:
                wait(sx.at[j, :, columns], xsend.at[j])

        sized(order[j], body)

    for j in range(4):
        left(j)
    wait(p1y.at[pl.ds(0, 3)], p1sem.at[0])
    wait(p1x.at[pl.ds(0, 3)], p1sem.at[2])
    for i in range(ITERS):
        wait(cbuf.at[i], c1sem.at[0, i])
        wait(zbuf.at[i, pl.ds(0, 7)], zsem.at[0, i])
        if i < ITERS - 1:
            wait(cbuf.at[i], c2sem.at[0, i])
            wait(pbuf.at[i, pl.ds(0, 15)], psem.at[0, i])
    wait(pfin.at[0], fsem.at[0])
    wait(qfin.at[pl.ds(0, 15)], qsend.at[0])
    wait(qfin.at[pl.ds(0, 16)], qsend.at[1])


def factors(grad, error, q_init):
    dma = pltpu.SemaphoreType.DMA
    vmem = pltpu.VMEM
    return pl.pallas_call(
        power,
        name="factors",
        out_shape=(
            jax.ShapeDtypeStruct((RANK, COLS), F32),
            jax.ShapeDtypeStruct((RANK, LANE), F32),
            jax.ShapeDtypeStruct((ROWS, COLS), F32),
        ),
        in_specs=[pl.BlockSpec(memory_space=pltpu.HBM)] * 3,
        out_specs=(pl.BlockSpec(memory_space=vmem),) * 3,
        scratch_shapes=[
            vmem((ROWS, COLS), BF16),
            vmem((RANK, COLS), F32),
            vmem((4, 4, HALF, WIN), F32),
            vmem((4, TOP, WIN), F32),
            vmem((4, HALF - TOP, WIN), F32),
            vmem((4, HALF, WIN), F32),
            vmem((4, HALF, WIN), F32),
            vmem((3, HALF, WIN), F32),
            vmem((4 * SLOT, WIN), F32),
            vmem((4 * SLOT, WIN), BF16),
            vmem((4 * SLOT, WIN), BF16),
            vmem((4, RANK, LANE), F32),
            vmem((4, RANK, LANE), F32),
            vmem((ITERS, 2 * PART, LANE), F32),
            vmem((ITERS, PART, LANE), F32),
            vmem((ITERS, PART, LANE), F32),
            vmem((ITERS, 8, PART, LANE), F32),
            vmem((ITERS, 2 * PART, LANE), F32),
            vmem((ITERS, 2 * RANK, LANE), F32),
            vmem((ITERS, 16, 2 * RANK, LANE), F32),
            vmem((2, RANK, LANE), F32),
            vmem((32, PART, LANE), F32),
            dma((2 * len(STARTS) + 1,)),
            dma((4,)),
            dma((4, 4)),
            dma((6, 4)),
            dma((6, 4)),
            dma((3,)),
            dma((3,)),
            dma((4,)),
            dma((2, ITERS)),
            dma((2, ITERS)),
            dma((2, ITERS)),
            dma((2, ITERS)),
            dma((2,)),
            dma((2,)),
            dma((16,)),
            dma((16,)),
        ],
        compiler_params=pltpu.CompilerParams(
            collective_id=0, has_side_effects=True, vmem_limit_bytes=40 * 2**20
        ),
    )(*(pltpu.with_memory_space_constraint(a, pltpu.HBM) for a in (grad, error, q_init)))


PARTS = (2, 4, 8, 10, 10, 10, 10, 10, 6, 4)


def finish(p, q, m, decompressed, new_error, q_next, dbuf, ebuf, sem):
    copies = [pltpu.make_async_copy(q, q_next, sem.at[0])]
    copies[0].start()
    p_high, p_rest = two_terms(p[:, :ROWS])
    left = jnp.concatenate([p_high, p_high, p_rest, p_rest], axis=0).astype(BF16)
    start = 0
    for i, part in enumerate(PARTS):
        columns = pl.ds(start, part * LANE)
        start += part * LANE
        q_high, q_rest = two_terms(q[:, columns])
        right = jnp.concatenate([q_high, q_rest, q_high, q_rest], axis=0).astype(BF16)
        approx = lax.dot_general(
            left, right, (((0,), (0,)), ((), ())), preferred_element_type=F32
        )
        ebuf[:, columns] = m[:, columns] - approx
        copies.append(pltpu.make_async_copy(ebuf.at[:, columns], new_error.at[0, :, columns], sem.at[2 * i + 1]))
        copies[-1].start()
        dbuf[:, columns] = approx.astype(BF16)
        copies.append(pltpu.make_async_copy(dbuf.at[:, columns], decompressed.at[:, columns], sem.at[2 * i + 2]))
        copies[-1].start()
    for copy in copies:
        copy.wait()


def outputs(p_hat, q_sum, merged):
    return pl.pallas_call(
        finish,
        name="outputs",
        in_specs=[pl.BlockSpec(memory_space=pltpu.VMEM)] * 3,
        out_specs=(pl.BlockSpec(memory_space=pltpu.HBM),) * 3,
        out_shape=(
            jax.ShapeDtypeStruct((ROWS, COLS), BF16),
            jax.ShapeDtypeStruct((1, ROWS, COLS), F32),
            jax.ShapeDtypeStruct((RANK, COLS), F32),
        ),
        scratch_shapes=[
            pltpu.VMEM((ROWS, COLS), BF16),
            pltpu.VMEM((ROWS, COLS), F32),
            pltpu.SemaphoreType.DMA((2 * len(PARTS) + 1,)),
        ],
        compiler_params=pltpu.CompilerParams(vmem_limit_bytes=24 * 2**20),
    )(p_hat, q_sum, merged)


def local(grad, error, q_init):
    q_sum, p_hat, merged = factors(grad, error, q_init)
    return outputs(p_hat, q_sum, merged)


def solution(mesh):
    return jax.shard_map(
        local,
        mesh=mesh,
        in_specs=(P("dp", "tensor", None), P("dp", "tensor", None), P()),
        out_specs=(P("tensor", None), P("dp", "tensor", None), P()),
        check_vma=False,
    )
```
